32 devices in a mesh: parts: 2 (over x), loop: 16 (over z, y, core).
Axes of the slice: x: 2, y: 2, z: 4, core: 2. Of those that a mesh axis runs over, the one named last changes fastest.
Arguments:
- leaf_rows: bfloat16 [128, 8192], P(('parts', 'loop')), parts along dimension 0, may hold values from -6 to 6
- norm_gain: float32 [8192], replicated, may hold values from 0.5 to 1.5
- gate_weight: bfloat16 [16, 1024, 13312], P('loop'), may hold values from -0.0625 to 0.0625
- up_weight: bfloat16 [16, 1024, 13312], P('loop'), may hold values from -0.0625 to 0.0625
- down_weight: bfloat16 [16, 13312, 1024], P('loop'), may hold values from -0.0390625 to 0.0390625
Outputs:
- leaf_output: bfloat16 [128, 8192], P(('parts', 'loop')), parts along dimension 0
The draws below stay inside these ranges and needn't reach their ends.
There are 2 independent parts, one for each index of `parts`. The reference program is written for one: setup_inputs(seed, part) draws one part's arguments, and reference() takes and returns one part's arrays. A program takes and returns all parts, laid end to end along the dimension named above; an argument that names none is the same for every part. Nothing has to cross between parts.
All inputs are finite; a program needn't handle non-finite values.
Results may differ from the reference program's by a relative error of at most 0.0048.
Values may be sent and summed in bfloat16 or wider, within the bound.
A program may use at most 192 MiB of HBM per device.

```python
import jax
import jax.numpy as jnp
from jax import lax

D = 8192
FF = 26624
FEAT_GROUPS = 8
ROWS = 64
HID_GROUPS = 2
DF = 1024
FH = 13312
N_LOOP = 16


def level_of(own_key, dims, pieces, least, top_value):
    def one(dim, parts):
        draws = jax.random.uniform(jax.random.fold_in(jax.random.fold_in(own_key, 6), dim), (parts,), jnp.float32, least / len(pieces), top_value / len(pieces))
        return jnp.repeat(jnp.exp(draws), dims[dim] // parts).reshape((-1,) + (1,) * (len(dims) - dim - 1))

    loudness = one(*pieces[0])
    for cut in pieces[1:]:
        loudness = loudness * one(*cut)
    return loudness


def scatter_about(stream_key, shape, deviation, reach, shards=(), held_as=jnp.bfloat16):
    drawn = deviation * jax.random.normal(stream_key, shape, jnp.float32)
    if shards:
        drawn = drawn * level_of(stream_key, shape, shards, -0.22, 0.18)
    return jnp.clip(drawn, -reach, reach).astype(held_as)


def setup_inputs(seed: int = 0, part: int = 0) -> dict:
    seeds = jax.random.split(jax.random.key(seed), 6)
    own_keys = jax.random.split(jax.random.fold_in(seeds[5], part), 6)
    return {
        "leaf_rows": scatter_about(own_keys[0], (ROWS, D), 1.0, 6.0, ((0, 16),)),
        "norm_gain": jnp.clip(1.0 + 0.1 * jax.random.normal(seeds[1], (D,), jnp.float32), 0.5, 1.5),
        "gate_weight": scatter_about(seeds[2], (N_LOOP, DF, FH), D ** -0.5, 0.0625, ((0, 16),)),
        "up_weight": scatter_about(seeds[3], (N_LOOP, DF, FH), D ** -0.5, 0.0625, ((0, 16),)),
        "down_weight": scatter_about(seeds[4], (N_LOOP, FH, DF), FF ** -0.5, 0.0390625, ((0, 16),)),
    }


epsilon = 1e-05

def normalize(leaf_rows, norm_gain):
    values = leaf_rows.astype(jnp.float32)
    inverse = lax.rsqrt(lax.optimization_barrier(jnp.mean(values * values, axis=1, keepdims=True)) + epsilon)
    return (values * inverse * norm_gain.astype(jnp.float32)).astype(jnp.bfloat16)

def reference(leaf_rows, norm_gain, gate_weight, up_weight, down_weight):
    normed = normalize(leaf_rows, norm_gain)
    gate_blocks = gate_weight.reshape(HID_GROUPS, D, FH)
    up_blocks = up_weight.reshape(HID_GROUPS, D, FH)
    down_blocks = down_weight.reshape(HID_GROUPS, FEAT_GROUPS, FH, DF)

    def one_group(total, blocks):
        gate_part, up_part, down_part = blocks
        gate_sum = jnp.dot(normed, gate_part, preferred_element_type=jnp.float32)
        up_sum = jnp.dot(normed, up_part, preferred_element_type=jnp.float32)
        hidden = (jax.nn.silu(gate_sum) * up_sum).astype(jnp.bfloat16)
        down_rows = jnp.transpose(down_part, (1, 0, 2)).reshape(FH, D)
        return (total + jnp.dot(hidden, down_rows, preferred_element_type=jnp.float32), None)
    start = jnp.zeros((ROWS, D), jnp.float32)
    branch, unused = lax.scan(one_group, start, (gate_blocks, up_blocks, down_blocks))
    return (leaf_rows.astype(jnp.float32) + branch).astype(jnp.bfloat16)
```

```python
import functools

import jax
import jax.numpy as jnp
from jax import lax
from jax.experimental import pallas as pl
from jax.experimental.pallas import tpu as pltpu
from jax.sharding import PartitionSpec as P

FEAT_GROUPS = 8
CHUNK = 512
SKEWS = (0, 1, 3, 5, 7, 9, 10)
VMEM_BYTES = 60 * 2**20
MESH = pl.DeviceIdType.MESH

epsilon = 1e-05


def fused_kernel(
    sizes, leaf_ref, gain_ref, gate_hbm, up_hbm, down_hbm, out_ref,
    gate_v, up_v, down_v, x_send, x_recv, x_full, keep,
    s1, r1, s2, r2, s3, r3, hid, y_acc, y_send, y_recv,
    w_sem, send_sem, recv_sem, xs_sem, xr_sem, ys_sem, yr_sem,
):
    parts, count, own, width, half, chunk = sizes
    n = parts * count
    nch = half // chunk
    rows = own * n
    split = 16 // own
    w4 = width // split
    part = lax.axis_index("parts")
    place = lax.axis_index("loop")
    me = part * count + place
    b0 = lax.rem(place, 2)
    b1 = lax.rem(place // 2, 2)
    b2 = lax.rem(place // 4, 2)
    core_peer = place + 1 - 2 * b0
    h2, h4, h8 = rows // 2, rows // 4, rows // 8

    def device(index):
        return {"parts": index // count, "loop": lax.rem(index, count)}

    def bits(j):
        even = 1 - lax.rem(j, 2)
        odd = 1 - even
        first_bit = even * b1 + odd * b2
        second_bit = even * b2 + odd * b1
        first_peer = place + (even * 2 + odd * 4) * (1 - 2 * first_bit)
        second_peer = place + (even * 4 + odd * 2) * (1 - 2 * second_bit)
        return first_bit, second_bit, first_peer, second_peer

    def load_gate(j):
        cols = pl.ds(pl.multiple_of(part * half + j * chunk, 128), chunk)
        return (
            pltpu.make_async_copy(gate_hbm.at[0, :, cols], gate_v.at[j], w_sem.at[0, j]),
            pltpu.make_async_copy(up_hbm.at[0, :, cols], up_v.at[j], w_sem.at[1, j]),
        )

    def load_down(j):
        at = pl.ds(pl.multiple_of(part * half + j * chunk, 16), chunk)
        return pltpu.make_async_copy(down_hbm.at[0, at, :], down_v.at[j], w_sem.at[2, j])

    @pl.loop(0, nch)
    def _(j):
        for copy in load_gate(j):
            copy.start()

    @pl.loop(0, nch)
    def _(j):
        load_down(j).start()

    barrier = pltpu.get_barrier_semaphore()

    @pl.loop(1, n)
    def _(k):
        pl.semaphore_signal(
            barrier, inc=1, device_id=device(lax.rem(me + k, n)), device_id_type=MESH
        )

    values = leaf_ref[...].astype(jnp.float32)
    inverse = lax.rsqrt(jnp.mean(values * values, axis=1, keepdims=True) + epsilon)
    normed = values * inverse * gain_ref[...]
    for f in range(FEAT_GROUPS):
        piece = jnp.concatenate(
            [normed[:, f * width + c * w4 : f * width + (c + 1) * w4] for c in range(split)], axis=0
        )
        x_send[f] = piece.astype(jnp.bfloat16)
    y_acc[...] = jnp.zeros_like(y_acc)
    x_recv[me] = x_send[lax.rem(place, FEAT_GROUPS)]

    pl.semaphore_wait(barrier, n - 1)

    def x_copy(to, source):
        return pltpu.make_async_remote_copy(
            src_ref=x_send.at[lax.rem(to, FEAT_GROUPS)],
            dst_ref=x_recv.at[source],
            send_sem=xs_sem.at[to],
            recv_sem=xr_sem.at[source],
            device_id=device(to),
            device_id_type=MESH,
        )

    @pl.loop(1, n)
    def _(k):
        x_copy(lax.rem(me + k, n), me).start()

    @pl.loop(1, n)
    def _(k):
        other = lax.rem(me + k, n)
        x_copy(other, other).wait_recv()

    group = 16 // own
    for t in range(rows // 16):
        base = lax.rem(t + b0 * (rows // 32), rows // 16) * group
        held = [x_recv[base + s].astype(jnp.float32) for s in range(group)]
        for c in range(split):
            tile = jnp.concatenate([h[c * own : (c + 1) * own] for h in held], axis=0)
            x_full[pl.ds(t * 16, 16), pl.ds(c * w4, w4)] = tile.astype(jnp.bfloat16)

    def remote(stage, j, src, dst, peer):
        return pltpu.make_async_remote_copy(
            src_ref=src,
            dst_ref=dst,
            send_sem=send_sem.at[stage, j],
            recv_sem=recv_sem.at[stage, j],
            device_id={"parts": part, "loop": peer},
            device_id_type=MESH,
        )

    def sixteen(value):
        return pl.multiple_of(value, 16)

    def copy_of(stage, j):
        fb, sb, fp, sp = bits(j)
        if stage == 0:
            return remote(0, j, s1.at[j], r1.at[j], core_peer)
        if stage == 1:
            return remote(1, j, s2.at[j], r2.at[j], fp)
        if stage == 2:
            return remote(2, j, s3.at[j], r3.at[j], sp)
        if stage == 3:
            at = hid.at[j, pl.ds(sixteen(b0 * h2 + fb * h4 + sb * h8), h8), :]
            return remote(3, j, at, at, sp)
        if stage == 4:
            at = hid.at[j, pl.ds(sixteen(b0 * h2 + fb * h4), h4), :]
            return remote(4, j, at, at, fp)
        at = hid.at[j, pl.ds(sixteen(b0 * h2), h2), :]
        return remote(5, j, at, at, core_peer)

    def arrival(stage, j):
        fb, sb, fp, sp = bits(j)
        if stage < 3:
            return copy_of(stage, j)
        if stage == 3:
            at = hid.at[j, pl.ds(sixteen(b0 * h2 + fb * h4 + (1 - sb) * h8), h8), :]
            return remote(3, j, at, at, sp)
        if stage == 4:
            at = hid.at[j, pl.ds(sixteen(b0 * h2 + (1 - fb) * h4), h4), :]
            return remote(4, j, at, at, fp)
        at = hid.at[j, pl.ds(sixteen((1 - b0) * h2), h2), :]
        return remote(5, j, at, at, core_peer)

    def project(j):
        for copy in load_gate(j):
            copy.wait()
        for at, weight in ((0, gate_v), (chunk, up_v)):
            both = jnp.dot(x_full[...], weight[j], preferred_element_type=jnp.float32)
            keep[j, :, pl.ds(at, chunk)] = both[:h2]
            s1[j, :, pl.ds(at, chunk)] = both[h2:].astype(jnp.bfloat16)
        copy_of(0, j).start()

    def partial(j, at, size):
        at = pl.ds(sixteen(at), size)
        return keep[j, at, :] + r1[j, at, :].astype(jnp.float32)

    def after_core(j):
        arrival(0, j).wait_recv()
        fb, sb, fp, sp = bits(j)
        s2[j] = partial(j, (1 - fb) * h4, h4).astype(jnp.bfloat16)
        copy_of(1, j).start()

    def after_first(j):
        arrival(1, j).wait_recv()
        fb, sb, fp, sp = bits(j)
        total = partial(j, fb * h4 + (1 - sb) * h8, h8)
        total += r2[j, pl.ds(sixteen((1 - sb) * h8), h8), :].astype(jnp.float32)
        s3[j] = total.astype(jnp.bfloat16)
        copy_of(2, j).start()

    def after_second(j):
        fb, sb, fp, sp = bits(j)
        total = partial(j, fb * h4 + sb * h8, h8)
        total += r2[j, pl.ds(sixteen(sb * h8), h8), :].astype(jnp.float32)
        arrival(2, j).wait_recv()
        total += r3[j].astype(jnp.float32)
        gate, up = total[:, :chunk], total[:, chunk:]
        hidden = gate / (1.0 + jnp.exp(-gate)) * up
        hid[j, pl.ds(sixteen(b0 * h2 + fb * h4 + sb * h8), h8), :] = hidden.astype(jnp.bfloat16)
        copy_of(3, j).start()

    def gather_first(j):
        arrival(3, j).wait_recv()
        copy_of(4, j).start()

    def gather_core(j):
        arrival(4, j).wait_recv()
        copy_of(5, j).start()

    def down(j):
        arrival(5, j).wait_recv()
        load_down(j).wait()
        y_acc[...] += jnp.dot(hid[j], down_v[j], preferred_element_type=jnp.float32)

    steps = (project, after_core, after_first, after_second, gather_first, gather_core, down)

    @pl.loop(0, nch + SKEWS[-1])
    def _(i):
        for at in (1, 2, 3, 4, 5, 0, 6):
            j = i - SKEWS[at]

            @pl.when((j >= 0) & (j < nch))
            def _():
                steps[at](j)

    @pl.loop(0, rows // 8)
    def _(t):
        block = y_acc[pl.ds(pl.multiple_of(t * 8, 8), 8), :]
        for s in range(8 // own):
            piece = jnp.concatenate(
                [block[s * own : (s + 1) * own, c * w4 : (c + 1) * w4] for c in range(split)], axis=0
            )
            y_send[t * (8 // own) + s] = piece.astype(jnp.bfloat16)

    def y_copy(to, source):
        return pltpu.make_async_remote_copy(
            src_ref=y_send.at[to],
            dst_ref=y_recv.at[source],
            send_sem=ys_sem.at[to],
            recv_sem=yr_sem.at[source],
            device_id=device(to),
            device_id_type=MESH,
        )

    @pl.loop(1, n)
    def _(k):
        y_copy(lax.rem(me + k, n), me).start()

    y_recv[me] = y_send[me]

    @pl.loop(1, n)
    def _(k):
        other = lax.rem(me + k, n)
        y_copy(other, other).wait_recv()

    for f in range(FEAT_GROUPS):
        branch = y_recv[f].astype(jnp.float32)
        for q in range(1, n // FEAT_GROUPS):
            branch += y_recv[q * FEAT_GROUPS + f].astype(jnp.float32)
        for c in range(split):
            at = f * width + c * w4
            rows_in = leaf_ref[:, at : at + w4].astype(jnp.float32)
            out_ref[:, at : at + w4] = (rows_in + branch[c * own : (c + 1) * own]).astype(jnp.bfloat16)

    @pl.loop(1, n)
    def _(k):
        other = lax.rem(me + k, n)
        x_copy(other, other).wait_send()
        y_copy(other, other).wait_send()

    @pl.loop(0, nch)
    def _(j):
        for stage in range(6):
            copy_of(stage, j).wait_send()


def fits(parts, count, own, width, hid_width, chunk):
    n = parts * count
    if own not in (2, 4, 8) or count % FEAT_GROUPS or hid_width % parts:
        return False
    half = hid_width // parts
    rows = own * n
    if half % chunk or rows % 128 or width % (16 // own * 128):
        return False
    need = half * width * 6 + half * rows * 12 + rows * width * 12
    return need < VMEM_BYTES * 0.95


def fused(parts, count, leaf_rows, norm_gain, gate_weight, up_weight, down_weight):
    own, features = leaf_rows.shape
    unused, width, hid_width = gate_weight.shape
    half = hid_width // parts
    chunk = CHUNK
    nch = half // chunk
    n = parts * count
    rows = own * n
    w4 = width // (16 // own)
    bf16, f32 = jnp.bfloat16, jnp.float32
    vmem = pl.BlockSpec(memory_space=pltpu.VMEM)
    hbm = pl.BlockSpec(memory_space=pl.ANY)
    dma = pltpu.SemaphoreType.DMA
    return pl.pallas_call(
        functools.partial(fused_kernel, (parts, count, own, width, half, chunk)),
        out_shape=jax.ShapeDtypeStruct((own, features), bf16),
        in_specs=[vmem, vmem, hbm, hbm, hbm],
        out_specs=vmem,
        scratch_shapes=[
            pltpu.VMEM((nch, width, chunk), bf16),
            pltpu.VMEM((nch, width, chunk), bf16),
            pltpu.VMEM((nch, chunk, width), bf16),
            pltpu.VMEM((FEAT_GROUPS, 16, w4), bf16),
            pltpu.VMEM((n, 16, w4), bf16),
            pltpu.VMEM((rows, width), bf16),
            pltpu.VMEM((nch, rows // 2, 2 * chunk), f32),
            pltpu.VMEM((nch, rows // 2, 2 * chunk), bf16),
            pltpu.VMEM((nch, rows // 2, 2 * chunk), bf16),
            pltpu.VMEM((nch, rows // 4, 2 * chunk), bf16),
            pltpu.VMEM((nch, rows // 4, 2 * chunk), bf16),
            pltpu.VMEM((nch, rows // 8, 2 * chunk), bf16),
            pltpu.VMEM((nch, rows // 8, 2 * chunk), bf16),
            pltpu.VMEM((nch, rows, chunk), bf16),
            pltpu.VMEM((rows, width), f32),
            pltpu.VMEM((n, 16, w4), bf16),
            pltpu.VMEM((n, 16, w4), bf16),
            dma((3, nch)),
            dma((6, nch)),
            dma((6, nch)),
            dma((n,)),
            dma((n,)),
            dma((n,)),
            dma((n,)),
        ],
        compiler_params=pltpu.CompilerParams(
            collective_id=0, has_side_effects=True, vmem_limit_bytes=VMEM_BYTES
        ),
    )(leaf_rows, norm_gain.reshape(1, features), gate_weight, up_weight, down_weight)


def swapped(value, axis, apart):
    mask = 2**apart
    pairs = [(source, source ^ mask) for source in range(lax.axis_size(axis))]
    return lax.ppermute(value, axis, pairs)


def normalize(leaf_rows, norm_gain):
    values = leaf_rows.astype(jnp.float32)
    inverse = lax.rsqrt(jnp.mean(values * values, axis=1, keepdims=True) + epsilon)
    return (values * inverse * norm_gain).astype(jnp.bfloat16)


def plain(leaf_rows, norm_gain, gate_weight, up_weight, down_weight):
    gate_block = gate_weight[0]
    up_block = up_weight[0]
    down_block = down_weight[0]
    width = gate_block.shape[0]
    hid_width = gate_block.shape[1]
    groups = FEAT_GROUPS
    own_rows = leaf_rows.shape[0]
    place = lax.axis_index("loop")
    count = lax.axis_size("loop")
    nbits = count.bit_length() - 1
    feat = place % groups
    normed = normalize(leaf_rows, norm_gain)
    row_slice = lax.dynamic_slice_in_dim(
        lax.all_gather(normed, "loop", axis=0, tiled=True), feat * width, width, 1
    )
    gate_sum = jnp.dot(row_slice, gate_block, preferred_element_type=jnp.float32)
    up_sum = jnp.dot(row_slice, up_block, preferred_element_type=jnp.float32)
    both = jnp.concatenate([gate_sum, up_sum], axis=1)
    current = both
    for bit in (2, 1, 0):
        half = current.shape[0] // 2
        mine = place // (1 << bit) % 2
        keep = lax.dynamic_slice_in_dim(current, mine * half, half, 0)
        other = lax.dynamic_slice_in_dim(current, (1 - mine) * half, half, 0)
        current = keep + swapped(other, "loop", bit)
    hidden = (jax.nn.silu(current[:, :hid_width]) * current[:, hid_width:]).astype(jnp.bfloat16)
    for bit in (0, 1, 2):
        mine = place // (1 << bit) % 2
        received = swapped(hidden, "loop", bit)
        hidden = jnp.where(
            mine == 0,
            jnp.concatenate([hidden, received], 0),
            jnp.concatenate([received, hidden], 0),
        )
    current = jnp.dot(hidden, down_block, preferred_element_type=jnp.float32)
    for bit in range(nbits - 1, 2, -1):
        half = current.shape[0] // 2
        mine = place // (1 << bit) % 2
        keep = lax.dynamic_slice_in_dim(current, mine * half, half, 0)
        other = lax.dynamic_slice_in_dim(current, (1 - mine) * half, half, 0)
        current = keep + swapped(other, "loop", bit)
    pieces = current.reshape(2, 2, 2, own_rows, width)
    for bit in (0, 1, 2):
        where_axis = 2 - bit
        mine = place // (1 << bit) % 2
        keep = lax.dynamic_index_in_dim(pieces, mine, where_axis, keepdims=False)
        other = lax.dynamic_index_in_dim(pieces, 1 - mine, where_axis, keepdims=False)
        received = swapped(other, "loop", bit)
        pieces = jnp.where(
            mine == 0,
            jnp.stack([keep, received], where_axis),
            jnp.stack([received, keep], where_axis),
        )
    branch = jnp.transpose(pieces.reshape(groups, own_rows, width), (1, 0, 2)).reshape(
        own_rows, groups * width
    )
    return (leaf_rows.astype(jnp.float32) + branch).astype(jnp.bfloat16)


def solution(mesh):
    parts, count = mesh.shape["parts"], mesh.shape["loop"]

    def per_device(leaf_rows, norm_gain, gate_weight, up_weight, down_weight):
        arrays = (leaf_rows, norm_gain, gate_weight, up_weight, down_weight)
        unused, width, hid_width = gate_weight.shape
        if fits(parts, count, leaf_rows.shape[0], width, hid_width, CHUNK):
            return fused(parts, count, *arrays)
        return plain(*arrays)

    return jax.shard_map(
        per_device,
        mesh=mesh,
        in_specs=(
            P(("parts", "loop"), None),
            P(),
            P("loop", None, None),
            P("loop", None, None),
            P("loop", None, None),
        ),
        out_specs=P(("parts", "loop"), None),
        check_vma=False,
    )
```

```python
import functools

import jax
import jax.numpy as jnp
from jax import lax
from jax.experimental import pallas as pl
from jax.experimental.pallas import tpu as pltpu
from jax.sharding import PartitionSpec as P

FEAT_GROUPS = 8
CHUNK = 512
SKEWS = (0, 4, 9, 14, 19, 24, 26)
VMEM_BYTES = 60 * 2**20
MESH = pl.DeviceIdType.MESH

epsilon = 1e-05


def fused_kernel(
    sizes, leaf_ref, gain_ref, gate_hbm, up_hbm, down_hbm, out_ref,
    gate_v, up_v, down_v, x_send, x_recv, x_full, keep,
    s1, r1, s2, r2, s3, r3, hid, y_acc, y_send, y_recv,
    y_far,
    w_sem, send_sem, recv_sem, xs_sem, xr_sem, ys_sem, yr_sem, block_sem,
):
    parts, count, own, width, half, chunk = sizes
    n = parts * count
    nch = half // chunk
    rows = own * n
    split = 16 // own
    w4 = width // split
    part = lax.axis_index("parts")
    place = lax.axis_index("loop")
    me = part * count + place
    b0 = lax.rem(place, 2)
    b1 = lax.rem(place // 2, 2)
    b2 = lax.rem(place // 4, 2)
    core_peer = place + 1 - 2 * b0
    h2, h4, h8 = rows // 2, rows // 4, rows // 8

    def device(index):
        return {"parts": index // count, "loop": lax.rem(index, count)}

    feat = lax.rem(place, FEAT_GROUPS)
    near_base = place - feat
    far_base = FEAT_GROUPS - near_base
    far_mine = part * count + far_base
    far_other = (1 - part) * count + far_base

    def near(k):
        inner = lax.rem(part * FEAT_GROUPS + feat + k, 2 * FEAT_GROUPS)
        return inner // FEAT_GROUPS * count + near_base + lax.rem(inner, FEAT_GROUPS)

    def far(k):
        return far_mine + lax.rem(feat + k, FEAT_GROUPS)

    some = FEAT_GROUPS // 2

    def across(k):
        return far_other + lax.rem(feat + k, FEAT_GROUPS)

    def bits(j):
        even = 1 - lax.rem(j, 2)
        odd = 1 - even
        first_bit = even * b1 + odd * b2
        second_bit = even * b2 + odd * b1
        first_peer = place + (even * 2 + odd * 4) * (1 - 2 * first_bit)
        second_peer = place + (even * 4 + odd * 2) * (1 - 2 * second_bit)
        return first_bit, second_bit, first_peer, second_peer

    def load_gate(j):
        cols = pl.ds(pl.multiple_of(part * half + j * chunk, 128), chunk)
        return (
            pltpu.make_async_copy(gate_hbm.at[0, :, cols], gate_v.at[j], w_sem.at[0, j]),
            pltpu.make_async_copy(up_hbm.at[0, :, cols], up_v.at[j], w_sem.at[1, j]),
        )

    def load_down(j):
        at = pl.ds(pl.multiple_of(part * half + j * chunk, 16), chunk)
        return pltpu.make_async_copy(down_hbm.at[0, at, :], down_v.at[j], w_sem.at[2, j])

    @pl.loop(0, nch)
    def _(j):
        for copy in load_gate(j):
            copy.start()

    @pl.loop(0, nch)
    def _(j):
        load_down(j).start()

    barrier = pltpu.get_barrier_semaphore()

    def greet(other):
        pl.semaphore_signal(barrier, inc=1, device_id=device(other), device_id_type=MESH)

    @pl.loop(1, n)
    def _(k):
        greet(lax.rem(me + k, n))

    values = leaf_ref[...].astype(jnp.float32)
    inverse = lax.rsqrt(jnp.mean(values * values, axis=1, keepdims=True) + epsilon)
    normed = values * inverse * gain_ref[...]
    for f in range(FEAT_GROUPS):
        piece = jnp.concatenate(
            [normed[:, f * width + c * w4 : f * width + (c + 1) * w4] for c in range(split)], axis=0
        )
        x_send[f] = piece.astype(jnp.bfloat16)
    y_acc[...] = jnp.zeros_like(y_acc)
    y_recv[...] = jnp.zeros_like(y_recv)
    x_recv[me] = x_send[lax.rem(place, FEAT_GROUPS)]

    pl.semaphore_wait(barrier, n - 1)

    def x_copy(to, source):
        return pltpu.make_async_remote_copy(
            src_ref=x_send.at[lax.rem(to, FEAT_GROUPS)],
            dst_ref=x_recv.at[source],
            send_sem=xs_sem.at[to],
            recv_sem=xr_sem.at[source],
            device_id=device(to),
            device_id_type=MESH,
        )

    def x_forward(base):
        block = x_recv.at[pl.ds(base, some)]
        return pltpu.make_async_remote_copy(
            src_ref=block,
            dst_ref=block,
            send_sem=block_sem.at[0],
            recv_sem=block_sem.at[1],
            device_id={"parts": 1 - part, "loop": place},
            device_id_type=MESH,
        )

    @pl.loop(0, FEAT_GROUPS)
    def _(k):
        x_copy(far(k), me).start()

    @pl.when(feat >= some)
    def _():
        @pl.loop(0, FEAT_GROUPS)
        def _(k):
            x_copy(across(k), me).start()

    @pl.loop(1, 2 * FEAT_GROUPS)
    def _(k):
        x_copy(near(k), me).start()

    @pl.loop(0, some)
    def _(k):
        x_copy(far_mine + k, far_mine + k).wait_recv()

    x_forward(far_mine).start()

    @pl.loop(some, FEAT_GROUPS)
    def _(k):
        x_copy(far_mine + k, far_mine + k).wait_recv()
        x_copy(far_other + k, far_other + k).wait_recv()

    @pl.loop(1, 2 * FEAT_GROUPS)
    def _(k):
        x_copy(near(k), near(k)).wait_recv()

    x_forward(far_other).wait_recv()

    group = 16 // own
    for t in range(rows // 16):
        base = lax.rem(t + b0 * (rows // 32), rows // 16) * group
        held = [x_recv[base + s].astype(jnp.float32) for s in range(group)]
        for c in range(split):
            tile = jnp.concatenate([h[c * own : (c + 1) * own] for h in held], axis=0)
            x_full[pl.ds(t * 16, 16), pl.ds(c * w4, w4)] = tile.astype(jnp.bfloat16)

    def remote(stage, j, src, dst, peer):
        return pltpu.make_async_remote_copy(
            src_ref=src,
            dst_ref=dst,
            send_sem=send_sem.at[stage, j],
            recv_sem=recv_sem.at[stage, j],
            device_id={"parts": part, "loop": peer},
            device_id_type=MESH,
        )

    def sixteen(value):
        return pl.multiple_of(value, 16)

    def copy_of(stage, j):
        fb, sb, fp, sp = bits(j)
        if stage == 0:
            return remote(0, j, s1.at[j], r1.at[j], core_peer)
        if stage == 1:
            return remote(1, j, s2.at[j], r2.at[j], fp)
        if stage == 2:
            return remote(2, j, s3.at[j], r3.at[j], sp)
        if stage == 3:
            at = hid.at[j, pl.ds(sixteen(b0 * h2 + fb * h4 + sb * h8), h8), :]
            return remote(3, j, at, at, sp)
        if stage == 4:
            at = hid.at[j, pl.ds(sixteen(b0 * h2 + fb * h4), h4), :]
            return remote(4, j, at, at, fp)
        at = hid.at[j, pl.ds(sixteen(b0 * h2), h2), :]
        return remote(5, j, at, at, core_peer)

    def arrival(stage, j):
        fb, sb, fp, sp = bits(j)
        if stage < 3:
            return copy_of(stage, j)
        if stage == 3:
            at = hid.at[j, pl.ds(sixteen(b0 * h2 + fb * h4 + (1 - sb) * h8), h8), :]
            return remote(3, j, at, at, sp)
        if stage == 4:
            at = hid.at[j, pl.ds(sixteen(b0 * h2 + (1 - fb) * h4), h4), :]
            return remote(4, j, at, at, fp)
        at = hid.at[j, pl.ds(sixteen((1 - b0) * h2), h2), :]
        return remote(5, j, at, at, core_peer)

    def project(j):
        for copy in load_gate(j):
            copy.wait()
        for at, weight in ((0, gate_v), (chunk, up_v)):
            both = jnp.dot(x_full[...], weight[j], preferred_element_type=jnp.float32)
            keep[j, :, pl.ds(at, chunk)] = both[:h2]
            s1[j, :, pl.ds(at, chunk)] = both[h2:].astype(jnp.bfloat16)
        copy_of(0, j).start()

    def partial(j, at, size):
        at = pl.ds(sixteen(at), size)
        return keep[j, at, :] + r1[j, at, :].astype(jnp.float32)

    def after_core(j):
        arrival(0, j).wait_recv()
        fb, sb, fp, sp = bits(j)
        s2[j] = partial(j, (1 - fb) * h4, h4).astype(jnp.bfloat16)
        copy_of(1, j).start()

    def after_first(j):
        arrival(1, j).wait_recv()
        fb, sb, fp, sp = bits(j)
        total = partial(j, fb * h4 + (1 - sb) * h8, h8)
        total += r2[j, pl.ds(sixteen((1 - sb) * h8), h8), :].astype(jnp.float32)
        s3[j] = total.astype(jnp.bfloat16)
        copy_of(2, j).start()

    def after_second(j):
        fb, sb, fp, sp = bits(j)
        total = partial(j, fb * h4 + sb * h8, h8)
        total += r2[j, pl.ds(sixteen(sb * h8), h8), :].astype(jnp.float32)
        arrival(2, j).wait_recv()
        total += r3[j].astype(jnp.float32)
        gate, up = total[:, :chunk], total[:, chunk:]
        hidden = gate / (1.0 + jnp.exp(-gate)) * up
        hid[j, pl.ds(sixteen(b0 * h2 + fb * h4 + sb * h8), h8), :] = hidden.astype(jnp.bfloat16)
        copy_of(3, j).start()

    def gather_first(j):
        arrival(3, j).wait_recv()
        copy_of(4, j).start()

    def gather_core(j):
        arrival(4, j).wait_recv()
        copy_of(5, j).start()

    def down(j):
        arrival(5, j).wait_recv()
        load_down(j).wait()
        y_acc[...] += jnp.dot(hid[j], down_v[j], preferred_element_type=jnp.float32)

    steps = (project, after_core, after_first, after_second, gather_first, gather_core, down)

    @pl.loop(0, nch + SKEWS[-1])
    def _(i):
        for at in (1, 2, 3, 4, 5, 0, 6):
            j = i - SKEWS[at]

            @pl.when((j >= 0) & (j < nch))
            def _():
                steps[at](j)

    @pl.loop(0, rows // 8)
    def _(t):
        block = y_acc[pl.ds(pl.multiple_of(t * 8, 8), 8), :]
        for s in range(8 // own):
            piece = jnp.concatenate(
                [block[s * own : (s + 1) * own, c * w4 : (c + 1) * w4] for c in range(split)], axis=0
            )
            y_send[t * (8 // own) + s] = piece.astype(jnp.bfloat16)

    y_block = pltpu.make_async_remote_copy(
        src_ref=y_send.at[pl.ds(far_other, some)],
        dst_ref=y_far,
        send_sem=block_sem.at[2],
        recv_sem=block_sem.at[3],
        device_id={"parts": 1 - part, "loop": place},
        device_id_type=MESH,
    )
    y_block.start()

    def y_copy(to, source):
        return pltpu.make_async_remote_copy(
            src_ref=y_send.at[to],
            dst_ref=y_recv.at[source],
            send_sem=ys_sem.at[to],
            recv_sem=yr_sem.at[source],
            device_id=device(to),
            device_id_type=MESH,
        )

    @pl.loop(some, FEAT_GROUPS)
    def _(k):
        y_copy(far_mine + k, me).start()
        y_copy(far_other + k, me).start()

    @pl.loop(1, 2 * FEAT_GROUPS)
    def _(k):
        y_copy(near(k), me).start()

    y_recv[me] = y_send[me]
    mine = pl.ds(far_mine, some)
    y_block.wait_recv()
    both_parts = y_send[mine].astype(jnp.float32) + y_far[...].astype(jnp.float32)
    y_send[mine] = both_parts.astype(jnp.bfloat16)

    @pl.loop(0, some)
    def _(k):
        y_copy(far_mine + k, me).start()

    x_forward(far_mine).wait_send()
    y_block.wait_send()

    @pl.loop(0, FEAT_GROUPS)
    def _(k):
        x_copy(far(k), far(k)).wait_send()

    @pl.when(feat >= some)
    def _():
        @pl.loop(0, FEAT_GROUPS)
        def _(k):
            x_copy(across(k), across(k)).wait_send()

    @pl.loop(1, 2 * FEAT_GROUPS)
    def _(k):
        x_copy(near(k), near(k)).wait_send()
        y_copy(near(k), near(k)).wait_send()

    @pl.loop(0, nch)
    def _(j):
        for stage in range(6):
            copy_of(stage, j).wait_send()

    @pl.loop(1, 2 * FEAT_GROUPS)
    def _(k):
        y_copy(near(k), near(k)).wait_recv()

    @pl.loop(0, FEAT_GROUPS)
    def _(k):
        y_copy(far(k), far(k)).wait_recv()

    @pl.when(feat >= some)
    def _():
        @pl.loop(0, FEAT_GROUPS)
        def _(k):
            y_copy(across(k), across(k)).wait_recv()

    for f in range(FEAT_GROUPS):
        branch = y_recv[part * count + near_base + f].astype(jnp.float32)
        branch += y_recv[(1 - part) * count + near_base + f].astype(jnp.float32)
        branch += y_recv[far_mine + f].astype(jnp.float32)
        branch += y_recv[far_other + f].astype(jnp.float32)
        for c in range(split):
            at = f * width + c * w4
            rows_in = leaf_ref[:, at : at + w4].astype(jnp.float32)
            out_ref[:, at : at + w4] = (rows_in + branch[c * own : (c + 1) * own]).astype(jnp.bfloat16)

    @pl.loop(0, FEAT_GROUPS)
    def _(k):
        y_copy(far(k), far(k)).wait_send()

    @pl.loop(some, FEAT_GROUPS)
    def _(k):
        y_copy(far_other + k, far_other + k).wait_send()


def fits(parts, count, own, width, hid_width, chunk):
    n = parts * count
    if own not in (2, 4, 8) or count != 2 * FEAT_GROUPS or parts != 2 or hid_width % parts:
        return False
    half = hid_width // parts
    rows = own * n
    if half % chunk or rows % 128 or width % (16 // own * 128):
        return False
    need = half * width * 6 + half * rows * 12 + rows * width * 12
    return need < VMEM_BYTES * 0.95


def fused(parts, count, leaf_rows, norm_gain, gate_weight, up_weight, down_weight):
    own, features = leaf_rows.shape
    unused, width, hid_width = gate_weight.shape
    half = hid_width // parts
    chunk = CHUNK
    nch = half // chunk
    n = parts * count
    rows = own * n
    w4 = width // (16 // own)
    bf16, f32 = jnp.bfloat16, jnp.float32
    vmem = pl.BlockSpec(memory_space=pltpu.VMEM)
    hbm = pl.BlockSpec(memory_space=pl.ANY)
    dma = pltpu.SemaphoreType.DMA
    return pl.pallas_call(
        functools.partial(fused_kernel, (parts, count, own, width, half, chunk)),
        out_shape=jax.ShapeDtypeStruct((own, features), bf16),
        in_specs=[vmem, vmem, hbm, hbm, hbm],
        out_specs=vmem,
        scratch_shapes=[
            pltpu.VMEM((nch, width, chunk), bf16),
            pltpu.VMEM((nch, width, chunk), bf16),
            pltpu.VMEM((nch, chunk, width), bf16),
            pltpu.VMEM((FEAT_GROUPS, 16, w4), bf16),
            pltpu.VMEM((n, 16, w4), bf16),
            pltpu.VMEM((rows, width), bf16),
            pltpu.VMEM((nch, rows // 2, 2 * chunk), f32),
            pltpu.VMEM((nch, rows // 2, 2 * chunk), bf16),
            pltpu.VMEM((nch, rows // 2, 2 * chunk), bf16),
            pltpu.VMEM((nch, rows // 4, 2 * chunk), bf16),
            pltpu.VMEM((nch, rows // 4, 2 * chunk), bf16),
            pltpu.VMEM((nch, rows // 8, 2 * chunk), bf16),
            pltpu.VMEM((nch, rows // 8, 2 * chunk), bf16),
            pltpu.VMEM((nch, rows, chunk), bf16),
            pltpu.VMEM((rows, width), f32),
            pltpu.VMEM((n, 16, w4), bf16),
            pltpu.VMEM((n, 16, w4), bf16),
            pltpu.VMEM((FEAT_GROUPS // 2, 16, w4), bf16),
            dma((3, nch)),
            dma((6, nch)),
            dma((6, nch)),
            dma((n,)),
            dma((n,)),
            dma((n,)),
            dma((n,)),
            dma((4,)),
        ],
        compiler_params=pltpu.CompilerParams(
            collective_id=0, has_side_effects=True, vmem_limit_bytes=VMEM_BYTES
        ),
    )(leaf_rows, norm_gain.reshape(1, features), gate_weight, up_weight, down_weight)


def swapped(value, axis, apart):
    mask = 2**apart
    pairs = [(source, source ^ mask) for source in range(lax.axis_size(axis))]
    return lax.ppermute(value, axis, pairs)


def normalize(leaf_rows, norm_gain):
    values = leaf_rows.astype(jnp.float32)
    inverse = lax.rsqrt(jnp.mean(values * values, axis=1, keepdims=True) + epsilon)
    return (values * inverse * norm_gain).astype(jnp.bfloat16)


def plain(leaf_rows, norm_gain, gate_weight, up_weight, down_weight):
    gate_block = gate_weight[0]
    up_block = up_weight[0]
    down_block = down_weight[0]
    width = gate_block.shape[0]
    hid_width = gate_block.shape[1]
    groups = FEAT_GROUPS
    own_rows = leaf_rows.shape[0]
    place = lax.axis_index("loop")
    count = lax.axis_size("loop")
    nbits = count.bit_length() - 1
    feat = place % groups
    normed = normalize(leaf_rows, norm_gain)
    row_slice = lax.dynamic_slice_in_dim(
        lax.all_gather(normed, "loop", axis=0, tiled=True), feat * width, width, 1
    )
    gate_sum = jnp.dot(row_slice, gate_block, preferred_element_type=jnp.float32)
    up_sum = jnp.dot(row_slice, up_block, preferred_element_type=jnp.float32)
    both = jnp.concatenate([gate_sum, up_sum], axis=1)
    current = both
    for bit in (2, 1, 0):
        half = current.shape[0] // 2
        mine = place // (1 << bit) % 2
        keep = lax.dynamic_slice_in_dim(current, mine * half, half, 0)
        other = lax.dynamic_slice_in_dim(current, (1 - mine) * half, half, 0)
        current = keep + swapped(other, "loop", bit)
    hidden = (jax.nn.silu(current[:, :hid_width]) * current[:, hid_width:]).astype(jnp.bfloat16)
    for bit in (0, 1, 2):
        mine = place // (1 << bit) % 2
        received = swapped(hidden, "loop", bit)
        hidden = jnp.where(
            mine == 0,
            jnp.concatenate([hidden, received], 0),
            jnp.concatenate([received, hidden], 0),
        )
    current = jnp.dot(hidden, down_block, preferred_element_type=jnp.float32)
    for bit in range(nbits - 1, 2, -1):
        half = current.shape[0] // 2
        mine = place // (1 << bit) % 2
        keep = lax.dynamic_slice_in_dim(current, mine * half, half, 0)
        other = lax.dynamic_slice_in_dim(current, (1 - mine) * half, half, 0)
        current = keep + swapped(other, "loop", bit)
    pieces = current.reshape(2, 2, 2, own_rows, width)
    for bit in (0, 1, 2):
        where_axis = 2 - bit
        mine = place // (1 << bit) % 2
        keep = lax.dynamic_index_in_dim(pieces, mine, where_axis, keepdims=False)
        other = lax.dynamic_index_in_dim(pieces, 1 - mine, where_axis, keepdims=False)
        received = swapped(other, "loop", bit)
        pieces = jnp.where(
            mine == 0,
            jnp.stack([keep, received], where_axis),
            jnp.stack([received, keep], where_axis),
        )
    branch = jnp.transpose(pieces.reshape(groups, own_rows, width), (1, 0, 2)).reshape(
        own_rows, groups * width
    )
    return (leaf_rows.astype(jnp.float32) + branch).astype(jnp.bfloat16)


def solution(mesh):
    parts, count = mesh.shape["parts"], mesh.shape["loop"]

    def per_device(leaf_rows, norm_gain, gate_weight, up_weight, down_weight):
        arrays = (leaf_rows, norm_gain, gate_weight, up_weight, down_weight)
        unused, width, hid_width = gate_weight.shape
        if fits(parts, count, leaf_rows.shape[0], width, hid_width, CHUNK):
            return fused(parts, count, *arrays)
        return plain(*arrays)

    return jax.shard_map(
        per_device,
        mesh=mesh,
        in_specs=(
            P(("parts", "loop"), None),
            P(),
            P("loop", None, None),
            P("loop", None, None),
            P("loop", None, None),
        ),
        out_specs=P(("parts", "loop"), None),
        check_vma=False,
    )
```

```python
import functools

import jax
import jax.numpy as jnp
from jax import lax
from jax.experimental import pallas as pl
from jax.experimental.pallas import tpu as pltpu
from jax.sharding import PartitionSpec as P

FEAT_GROUPS = 8
CHUNK = 512
SKEWS = (0, 4, 10, 17, 24, 31, 33)
VMEM_BYTES = 60 * 2**20
MESH = pl.DeviceIdType.MESH

epsilon = 1e-05


def fused_kernel(
    sizes, leaf_ref, gain_ref, gate_hbm, up_hbm, down_hbm, out_ref,
    gate_v, up_v, down_v, x_send, x_recv, x_full, keep,
    s1, r1, s2, r2, s3, r3, hid, y_acc, y_send, y_recv,
    y_far,
    w_sem, send_sem, recv_sem, xs_sem, xr_sem, ys_sem, yr_sem, block_sem,
):
    parts, count, own, width, half, chunk = sizes
    n = parts * count
    nch = half // chunk
    rows = own * n
    split = 16 // own
    w4 = width // split
    part = lax.axis_index("parts")
    place = lax.axis_index("loop")
    me = part * count + place
    b0 = lax.rem(place, 2)
    b1 = lax.rem(place // 2, 2)
    b2 = lax.rem(place // 4, 2)
    core_peer = place + 1 - 2 * b0
    h2, h4, h8 = rows // 2, rows // 4, rows // 8

    def device(index):
        return {"parts": index // count, "loop": lax.rem(index, count)}

    feat = lax.rem(place, FEAT_GROUPS)
    near_base = place - feat
    far_base = FEAT_GROUPS - near_base
    far_mine = part * count + far_base
    far_other = (1 - part) * count + far_base

    def near(k):
        inner = lax.rem(part * FEAT_GROUPS + feat + k, 2 * FEAT_GROUPS)
        return inner // FEAT_GROUPS * count + near_base + lax.rem(inner, FEAT_GROUPS)

    def far(k):
        return far_mine + lax.rem(feat + k, FEAT_GROUPS)

    some = FEAT_GROUPS // 2

    def across(k):
        return far_other + lax.rem(feat + k, FEAT_GROUPS)

    def bits(j):
        even = 1 - lax.rem(j, 2)
        odd = 1 - even
        first_bit = even * b1 + odd * b2
        second_bit = even * b2 + odd * b1
        first_peer = place + (even * 2 + odd * 4) * (1 - 2 * first_bit)
        second_peer = place + (even * 4 + odd * 2) * (1 - 2 * second_bit)
        return first_bit, second_bit, first_peer, second_peer

    def load_gate(j):
        cols = pl.ds(pl.multiple_of(part * half + j * chunk, 128), chunk)
        return (
            pltpu.make_async_copy(gate_hbm.at[0, :, cols], gate_v.at[j], w_sem.at[0, j]),
            pltpu.make_async_copy(up_hbm.at[0, :, cols], up_v.at[j], w_sem.at[1, j]),
        )

    def load_down(j):
        at = pl.ds(pl.multiple_of(part * half + j * chunk, 16), chunk)
        return pltpu.make_async_copy(down_hbm.at[0, at, :], down_v.at[j], w_sem.at[2, j])

    @pl.loop(0, nch)
    def _(j):
        for copy in load_gate(j):
            copy.start()

    @pl.loop(0, nch)
    def _(j):
        load_down(j).start()

    barrier = pltpu.get_barrier_semaphore()

    def greet(other):
        pl.semaphore_signal(barrier, inc=1, device_id=device(other), device_id_type=MESH)

    @pl.loop(1, n)
    def _(k):
        greet(lax.rem(me + k, n))

    values = leaf_ref[...].astype(jnp.float32)
    inverse = lax.rsqrt(jnp.mean(values * values, axis=1, keepdims=True) + epsilon)
    normed = values * inverse * gain_ref[...]
    for f in range(FEAT_GROUPS):
        piece = jnp.concatenate(
            [normed[:, f * width + c * w4 : f * width + (c + 1) * w4] for c in range(split)], axis=0
        )
        x_send[f] = piece.astype(jnp.bfloat16)
    y_acc[...] = jnp.zeros_like(y_acc)
    y_recv[...] = jnp.zeros_like(y_recv)
    x_recv[me] = x_send[lax.rem(place, FEAT_GROUPS)]

    pl.semaphore_wait(barrier, n - 1)

    def x_copy(to, source):
        return pltpu.make_async_remote_copy(
            src_ref=x_send.at[lax.rem(to, FEAT_GROUPS)],
            dst_ref=x_recv.at[source],
            send_sem=xs_sem.at[to],
            recv_sem=xr_sem.at[source],
            device_id=device(to),
            device_id_type=MESH,
        )

    def x_forward(base):
        block = x_recv.at[pl.ds(base, some)]
        return pltpu.make_async_remote_copy(
            src_ref=block,
            dst_ref=block,
            send_sem=block_sem.at[0],
            recv_sem=block_sem.at[1],
            device_id={"parts": 1 - part, "loop": place},
            device_id_type=MESH,
        )

    @pl.loop(0, FEAT_GROUPS)
    def _(k):
        x_copy(far(k), me).start()

    @pl.when(feat >= some)
    def _():
        @pl.loop(0, FEAT_GROUPS)
        def _(k):
            x_copy(across(k), me).start()

    @pl.loop(1, 2 * FEAT_GROUPS)
    def _(k):
        x_copy(near(k), me).start()

    @pl.loop(0, some)
    def _(k):
        x_copy(far_mine + k, far_mine + k).wait_recv()

    x_forward(far_mine).start()

    @pl.loop(some, FEAT_GROUPS)
    def _(k):
        x_copy(far_mine + k, far_mine + k).wait_recv()
        x_copy(far_other + k, far_other + k).wait_recv()

    @pl.loop(1, 2 * FEAT_GROUPS)
    def _(k):
        x_copy(near(k), near(k)).wait_recv()

    x_forward(far_other).wait_recv()

    group = 16 // own
    for t in range(rows // 16):
        base = lax.rem(t + b0 * (rows // 32), rows // 16) * group
        held = [x_recv[base + s].astype(jnp.float32) for s in range(group)]
        for c in range(split):
            tile = jnp.concatenate([h[c * own : (c + 1) * own] for h in held], axis=0)
            x_full[pl.ds(t * 16, 16), pl.ds(c * w4, w4)] = tile.astype(jnp.bfloat16)

    def remote(stage, j, src, dst, peer):
        return pltpu.make_async_remote_copy(
            src_ref=src,
            dst_ref=dst,
            send_sem=send_sem.at[stage, j],
            recv_sem=recv_sem.at[stage, j],
            device_id={"parts": part, "loop": peer},
            device_id_type=MESH,
        )

    def sixteen(value):
        return pl.multiple_of(value, 16)

    def copy_of(stage, j):
        fb, sb, fp, sp = bits(j)
        if stage == 0:
            return remote(0, j, s1.at[j], r1.at[j], core_peer)
        if stage == 1:
            return remote(1, j, s2.at[j], r2.at[j], fp)
        if stage == 2:
            return remote(2, j, s3.at[j], r3.at[j], sp)
        if stage == 3:
            at = hid.at[j, pl.ds(sixteen(b0 * h2 + fb * h4 + sb * h8), h8), :]
            return remote(3, j, at, at, sp)
        if stage == 4:
            at = hid.at[j, pl.ds(sixteen(b0 * h2 + fb * h4), h4), :]
            return remote(4, j, at, at, fp)
        at = hid.at[j, pl.ds(sixteen(b0 * h2), h2), :]
        return remote(5, j, at, at, core_peer)

    def arrival(stage, j):
        fb, sb, fp, sp = bits(j)
        if stage < 3:
            return copy_of(stage, j)
        if stage == 3:
            at = hid.at[j, pl.ds(sixteen(b0 * h2 + fb * h4 + (1 - sb) * h8), h8), :]
            return remote(3, j, at, at, sp)
        if stage == 4:
            at = hid.at[j, pl.ds(sixteen(b0 * h2 + (1 - fb) * h4), h4), :]
            return remote(4, j, at, at, fp)
        at = hid.at[j, pl.ds(sixteen((1 - b0) * h2), h2), :]
        return remote(5, j, at, at, core_peer)

    def project(j):
        for copy in load_gate(j):
            copy.wait()
        for at, weight in ((0, gate_v), (chunk, up_v)):
            both = jnp.dot(x_full[...], weight[j], preferred_element_type=jnp.float32)
            keep[j, :, pl.ds(at, chunk)] = both[:h2]
            s1[j, :, pl.ds(at, chunk)] = both[h2:].astype(jnp.bfloat16)
        copy_of(0, j).start()

    def partial(j, at, size):
        at = pl.ds(sixteen(at), size)
        return keep[j, at, :] + r1[j, at, :].astype(jnp.float32)

    def after_core(j):
        arrival(0, j).wait_recv()
        fb, sb, fp, sp = bits(j)
        s2[j] = partial(j, (1 - fb) * h4, h4).astype(jnp.bfloat16)
        copy_of(1, j).start()

    def after_first(j):
        arrival(1, j).wait_recv()
        fb, sb, fp, sp = bits(j)
        total = partial(j, fb * h4 + (1 - sb) * h8, h8)
        total += r2[j, pl.ds(sixteen((1 - sb) * h8), h8), :].astype(jnp.float32)
        s3[j] = total.astype(jnp.bfloat16)
        copy_of(2, j).start()

    def after_second(j):
        fb, sb, fp, sp = bits(j)
        total = partial(j, fb * h4 + sb * h8, h8)
        total += r2[j, pl.ds(sixteen(sb * h8), h8), :].astype(jnp.float32)
        arrival(2, j).wait_recv()
        total += r3[j].astype(jnp.float32)
        gate, up = total[:, :chunk], total[:, chunk:]
        hidden = gate / (1.0 + jnp.exp(-gate)) * up
        hid[j, pl.ds(sixteen(b0 * h2 + fb * h4 + sb * h8), h8), :] = hidden.astype(jnp.bfloat16)
        copy_of(3, j).start()

    def gather_first(j):
        arrival(3, j).wait_recv()
        copy_of(4, j).start()

    def gather_core(j):
        arrival(4, j).wait_recv()
        copy_of(5, j).start()

    def down(j):
        arrival(5, j).wait_recv()
        load_down(j).wait()
        y_acc[...] += jnp.dot(hid[j], down_v[j], preferred_element_type=jnp.float32)

    steps = (project, after_core, after_first, after_second, gather_first, gather_core, down)

    @pl.loop(0, nch + SKEWS[-1])
    def _(i):
        for at in (1, 2, 3, 4, 5, 0, 6):
            j = i - SKEWS[at]

            @pl.when((j >= 0) & (j < nch))
            def _():
                steps[at](j)

    @pl.loop(0, rows // 8)
    def _(t):
        block = y_acc[pl.ds(pl.multiple_of(t * 8, 8), 8), :]
        for s in range(8 // own):
            piece = jnp.concatenate(
                [block[s * own : (s + 1) * own, c * w4 : (c + 1) * w4] for c in range(split)], axis=0
            )
            y_send[t * (8 // own) + s] = piece.astype(jnp.bfloat16)

    y_block = pltpu.make_async_remote_copy(
        src_ref=y_send.at[pl.ds(far_other, some)],
        dst_ref=y_far,
        send_sem=block_sem.at[2],
        recv_sem=block_sem.at[3],
        device_id={"parts": 1 - part, "loop": place},
        device_id_type=MESH,
    )
    y_block.start()

    def y_copy(to, source):
        return pltpu.make_async_remote_copy(
            src_ref=y_send.at[to],
            dst_ref=y_recv.at[source],
            send_sem=ys_sem.at[to],
            recv_sem=yr_sem.at[source],
            device_id=device(to),
            device_id_type=MESH,
        )

    @pl.loop(some, FEAT_GROUPS)
    def _(k):
        y_copy(far_mine + k, me).start()
        y_copy(far_other + k, me).start()

    @pl.loop(1, 2 * FEAT_GROUPS)
    def _(k):
        y_copy(near(k), me).start()

    y_recv[me] = y_send[me]
    mine = pl.ds(far_mine, some)
    y_block.wait_recv()
    both_parts = y_send[mine].astype(jnp.float32) + y_far[...].astype(jnp.float32)
    y_send[mine] = both_parts.astype(jnp.bfloat16)

    @pl.loop(0, some)
    def _(k):
        y_copy(far_mine + k, me).start()

    x_forward(far_mine).wait_send()
    y_block.wait_send()

    @pl.loop(0, FEAT_GROUPS)
    def _(k):
        x_copy(far(k), far(k)).wait_send()

    @pl.when(feat >= some)
    def _():
        @pl.loop(0, FEAT_GROUPS)
        def _(k):
            x_copy(across(k), across(k)).wait_send()

    @pl.loop(1, 2 * FEAT_GROUPS)
    def _(k):
        x_copy(near(k), near(k)).wait_send()
        y_copy(near(k), near(k)).wait_send()

    @pl.loop(0, nch)
    def _(j):
        for stage in range(6):
            copy_of(stage, j).wait_send()

    @pl.loop(1, 2 * FEAT_GROUPS)
    def _(k):
        y_copy(near(k), near(k)).wait_recv()

    @pl.loop(0, FEAT_GROUPS)
    def _(k):
        y_copy(far(k), far(k)).wait_recv()

    @pl.when(feat >= some)
    def _():
        @pl.loop(0, FEAT_GROUPS)
        def _(k):
            y_copy(across(k), across(k)).wait_recv()

    for f in range(FEAT_GROUPS):
        branch = y_recv[part * count + near_base + f].astype(jnp.float32)
        branch += y_recv[(1 - part) * count + near_base + f].astype(jnp.float32)
        branch += y_recv[far_mine + f].astype(jnp.float32)
        branch += y_recv[far_other + f].astype(jnp.float32)
        for c in range(split):
            at = f * width + c * w4
            rows_in = leaf_ref[:, at : at + w4].astype(jnp.float32)
            out_ref[:, at : at + w4] = (rows_in + branch[c * own : (c + 1) * own]).astype(jnp.bfloat16)

    @pl.loop(0, FEAT_GROUPS)
    def _(k):
        y_copy(far(k), far(k)).wait_send()

    @pl.loop(some, FEAT_GROUPS)
    def _(k):
        y_copy(far_other + k, far_other + k).wait_send()


def fits(parts, count, own, width, hid_width, chunk):
    n = parts * count
    if own not in (2, 4, 8) or count != 2 * FEAT_GROUPS or parts != 2 or hid_width % parts:
        return False
    half = hid_width // parts
    rows = own * n
    if half % chunk or rows % 128 or width % (16 // own * 128):
        return False
    need = half * width * 6 + half * rows * 12 + rows * width * 12
    return need < VMEM_BYTES * 0.95


def fused(parts, count, leaf_rows, norm_gain, gate_weight, up_weight, down_weight):
    own, features = leaf_rows.shape
    unused, width, hid_width = gate_weight.shape
    half = hid_width // parts
    chunk = CHUNK
    nch = half // chunk
    n = parts * count
    rows = own * n
    w4 = width // (16 // own)
    bf16, f32 = jnp.bfloat16, jnp.float32
    vmem = pl.BlockSpec(memory_space=pltpu.VMEM)
    hbm = pl.BlockSpec(memory_space=pl.ANY)
    dma = pltpu.SemaphoreType.DMA
    return pl.pallas_call(
        functools.partial(fused_kernel, (parts, count, own, width, half, chunk)),
        out_shape=jax.ShapeDtypeStruct((own, features), bf16),
        in_specs=[vmem, vmem, hbm, hbm, hbm],
        out_specs=vmem,
        scratch_shapes=[
            pltpu.VMEM((nch, width, chunk), bf16),
            pltpu.VMEM((nch, width, chunk), bf16),
            pltpu.VMEM((nch, chunk, width), bf16),
            pltpu.VMEM((FEAT_GROUPS, 16, w4), bf16),
            pltpu.VMEM((n, 16, w4), bf16),
            pltpu.VMEM((rows, width), bf16),
            pltpu.VMEM((nch, rows // 2, 2 * chunk), f32),
            pltpu.VMEM((nch, rows // 2, 2 * chunk), bf16),
            pltpu.VMEM((nch, rows // 2, 2 * chunk), bf16),
            pltpu.VMEM((nch, rows // 4, 2 * chunk), bf16),
            pltpu.VMEM((nch, rows // 4, 2 * chunk), bf16),
            pltpu.VMEM((nch, rows // 8, 2 * chunk), bf16),
            pltpu.VMEM((nch, rows // 8, 2 * chunk), bf16),
            pltpu.VMEM((nch, rows, chunk), bf16),
            pltpu.VMEM((rows, width), f32),
            pltpu.VMEM((n, 16, w4), bf16),
            pltpu.VMEM((n, 16, w4), bf16),
            pltpu.VMEM((FEAT_GROUPS // 2, 16, w4), bf16),
            dma((3, nch)),
            dma((6, nch)),
            dma((6, nch)),
            dma((n,)),
            dma((n,)),
            dma((n,)),
            dma((n,)),
            dma((4,)),
        ],
        compiler_params=pltpu.CompilerParams(
            collective_id=0, has_side_effects=True, vmem_limit_bytes=VMEM_BYTES
        ),
    )(leaf_rows, norm_gain.reshape(1, features), gate_weight, up_weight, down_weight)


def swapped(value, axis, apart):
    mask = 2**apart
    pairs = [(source, source ^ mask) for source in range(lax.axis_size(axis))]
    return lax.ppermute(value, axis, pairs)


def normalize(leaf_rows, norm_gain):
    values = leaf_rows.astype(jnp.float32)
    inverse = lax.rsqrt(jnp.mean(values * values, axis=1, keepdims=True) + epsilon)
    return (values * inverse * norm_gain).astype(jnp.bfloat16)


def plain(leaf_rows, norm_gain, gate_weight, up_weight, down_weight):
    gate_block = gate_weight[0]
    up_block = up_weight[0]
    down_block = down_weight[0]
    width = gate_block.shape[0]
    hid_width = gate_block.shape[1]
    groups = FEAT_GROUPS
    own_rows = leaf_rows.shape[0]
    place = lax.axis_index("loop")
    count = lax.axis_size("loop")
    nbits = count.bit_length() - 1
    feat = place % groups
    normed = normalize(leaf_rows, norm_gain)
    row_slice = lax.dynamic_slice_in_dim(
        lax.all_gather(normed, "loop", axis=0, tiled=True), feat * width, width, 1
    )
    gate_sum = jnp.dot(row_slice, gate_block, preferred_element_type=jnp.float32)
    up_sum = jnp.dot(row_slice, up_block, preferred_element_type=jnp.float32)
    both = jnp.concatenate([gate_sum, up_sum], axis=1)
    current = both
    for bit in (2, 1, 0):
        half = current.shape[0] // 2
        mine = place // (1 << bit) % 2
        keep = lax.dynamic_slice_in_dim(current, mine * half, half, 0)
        other = lax.dynamic_slice_in_dim(current, (1 - mine) * half, half, 0)
        current = keep + swapped(other, "loop", bit)
    hidden = (jax.nn.silu(current[:, :hid_width]) * current[:, hid_width:]).astype(jnp.bfloat16)
    for bit in (0, 1, 2):
        mine = place // (1 << bit) % 2
        received = swapped(hidden, "loop", bit)
        hidden = jnp.where(
            mine == 0,
            jnp.concatenate([hidden, received], 0),
            jnp.concatenate([received, hidden], 0),
        )
    current = jnp.dot(hidden, down_block, preferred_element_type=jnp.float32)
    for bit in range(nbits - 1, 2, -1):
        half = current.shape[0] // 2
        mine = place // (1 << bit) % 2
        keep = lax.dynamic_slice_in_dim(current, mine * half, half, 0)
        other = lax.dynamic_slice_in_dim(current, (1 - mine) * half, half, 0)
        current = keep + swapped(other, "loop", bit)
    pieces = current.reshape(2, 2, 2, own_rows, width)
    for bit in (0, 1, 2):
        where_axis = 2 - bit
        mine = place // (1 << bit) % 2
        keep = lax.dynamic_index_in_dim(pieces, mine, where_axis, keepdims=False)
        other = lax.dynamic_index_in_dim(pieces, 1 - mine, where_axis, keepdims=False)
        received = swapped(other, "loop", bit)
        pieces = jnp.where(
            mine == 0,
            jnp.stack([keep, received], where_axis),
            jnp.stack([received, keep], where_axis),
        )
    branch = jnp.transpose(pieces.reshape(groups, own_rows, width), (1, 0, 2)).reshape(
        own_rows, groups * width
    )
    return (leaf_rows.astype(jnp.float32) + branch).astype(jnp.bfloat16)


def solution(mesh):
    parts, count = mesh.shape["parts"], mesh.shape["loop"]

    def per_device(leaf_rows, norm_gain, gate_weight, up_weight, down_weight):
        arrays = (leaf_rows, norm_gain, gate_weight, up_weight, down_weight)
        unused, width, hid_width = gate_weight.shape
        if fits(parts, count, leaf_rows.shape[0], width, hid_width, CHUNK):
            return fused(parts, count, *arrays)
        return plain(*arrays)

    return jax.shard_map(
        per_device,
        mesh=mesh,
        in_specs=(
            P(("parts", "loop"), None),
            P(),
            P("loop", None, None),
            P("loop", None, None),
            P("loop", None, None),
        ),
        out_specs=P(("parts", "loop"), None),
        check_vma=False,
    )
```
